32 devices in a mesh: seq: 16 (over z, y, core), fsdp: 2 (over x).
Axes of the slice: x: 2, y: 2, z: 4, core: 2. Of those that a mesh axis runs over, the one named last changes fastest.
Arguments:
- dna_embed: bfloat16 [2, 4096, 1024], P('fsdp', 'seq'), may hold values from -60 to 60
- site_owner: int32 [2, 4096, 1], P('fsdp', 'seq'), may hold values from 0 to 15; in each aligned block of 256 rows (0 to 255, 256 to 511, ..., all dimensions but the last counted through in order) at most 32 rows name the same one
- site_row: int32 [2, 4096], P('fsdp', 'seq'), may hold values from 0 to 2047
- variant_table: bfloat16 [32768, 1024], P('seq'), may hold values from -6 to 6
- norm_gain: float32 [1024], replicated, may hold values from 0.1 to 1.9
- conv_weight: bfloat16 [7, 1024], replicated, may hold values from -2.390625 to 2.390625
- qkv_weight: bfloat16 [1024, 3072], P(None, 'fsdp'), may hold values from -4 to 4
- out_weight: bfloat16 [1024, 1024], P(None, 'fsdp'), may hold values from -0.1875 to 0.1875
- attn_gain: float32 [1024], replicated, may hold values from 0.1 to 1.9
Outputs:
- mixed: bfloat16 [2, 4096, 1024], P('fsdp', 'seq')
The draws below stay inside these ranges and needn't reach their ends.
Inputs may be any that keep to these rules, and one draw needn't show every extreme that they name: `site_owner`: in each haplotype the 256 positions of one device name one site range at most 32 times, and some site range exactly 32 times.
All inputs are finite; a program needn't handle non-finite values.
Results may differ from the reference program's by a relative error of at most 0.0075.
The reference program's roundings to bfloat16 on the way (of `site_embed`, `normed`, `conv_out`, `qkv`, `probs` and `attn_normed`) count: a program that leaves them out, or rounds other values in their place, can miss the bound.
Values may be sent and summed in bfloat16 or wider, within the bound.
A program may use at most 128 MiB of HBM per device.

```python
import math
import jax
import jax.numpy as jnp
import numpy as np
from jax import lax

D = 1024
HEADS = 16
HEAD = 64
CONV = 7
WINDOW = 2048
L_DEV = 256
SITES_DEV = 2048
HAPS = 2
SEQ = 4096
SITES = 32768
CAP = 32
N_SEQ = 16


def draw_dna_embed(key, part):
    key_base, key_rows, key_cols = jax.random.split(key, 3)
    shape = (HAPS, SEQ, D)
    base = jnp.clip(jax.random.normal(key_base, shape, jnp.float32), -6.0, 6.0)
    row_scale = jnp.exp(jax.random.uniform(key_rows, (HAPS, SEQ, 1), jnp.float32, 0.0, math.log(10.0)))
    col_scale = jnp.exp(jax.random.uniform(key_cols, (D,), jnp.float32, 0.0, math.log(10.0)))
    return (base * row_scale * col_scale * 0.1).astype(jnp.bfloat16)


def draw_qkv_weight(key, part):
    key_base = jax.random.fold_in(key, 0)
    base = jnp.clip(jax.random.normal(key_base, (D, 3 * D), jnp.float32), -6.0, 6.0) * D ** (-0.5)
    return base.astype(jnp.bfloat16)


def with_ends(entries, rng, low, top_value):
    extent = entries.shape
    index_at = [jax.random.randint(jax.random.fold_in(rng, axis), (), 0, extent[axis]) for axis in range(len(extent))]
    entries = entries.at[tuple(index_at)].set(low)
    longest = extent.index(max(extent))
    index_at[longest] = (index_at[longest] + 1) % extent[longest]
    return entries.at[tuple(index_at)].set(top_value)


def block_levels(key, dims, pieces, low, high):
    level, own = 1.0, jax.random.fold_in(key, 6)
    for position, blocks in pieces:
        draws = jnp.exp(jax.random.uniform(jax.random.fold_in(own, position), (blocks,), jnp.float32, low / len(pieces), high / len(pieces)))
        level = level * jnp.repeat(draws, dims[position] // blocks).reshape([-1 if axis == position else 1 for axis in range(len(dims))])
    return level


def routed_block(stream_key, own, number, rows, count, top, limit, lean):
    sequence = jax.random.permutation(stream_key, count)
    crowded, common = shares(count, rows * top, limit, lean, True), shares(count, rows * top, limit, lean, False)
    places = jnp.arange(count)

    def named(lengths, rotation):
        used = int((lengths > 0).sum())
        fixed = max(1, used // 4)
        passed = fixed + (places - fixed + rotation * (used - fixed)) % max(1, count - fixed)
        return jnp.zeros((count,), jnp.int32).at[sequence[jnp.where(places < fixed, places, passed)]].set(jnp.asarray(lengths, jnp.int32))

    lengths = jnp.where(number % 4 == 0, named(crowded, number // 4), named(common, number - number // 4 - 1))
    mixed = jax.random.permutation(jax.random.fold_in(own, 3), count)
    giver, sink = mixed[0:count // 2 * 2:2], mixed[1:count // 2 * 2:2]
    room = jnp.minimum(lengths[giver] - 1, limit - lengths[sink]) // 2
    room = jnp.where((giver == sequence[0]) | (sink == sequence[0]) | (lengths[sink] == 0), 0, jnp.maximum(room, 0))
    passed = jax.random.randint(jax.random.fold_in(own, 4), (count // 2,), 0, 1 << 20) % (room + 1)
    lengths = lengths.at[giver].add(-passed).at[sink].add(passed)
    members = jnp.searchsorted(jnp.cumsum(lengths), jnp.arange(rows * top), side="right").astype(jnp.int32)
    listing = members.reshape(top, rows).T
    listing = listing[jax.random.permutation(jax.random.fold_in(own, 1), rows)]
    rotation = jax.random.randint(jax.random.fold_in(own, 2), (rows, 1), 0, top)
    return jnp.take_along_axis(listing, (jnp.arange(top)[None, :] + rotation) % top, axis=1)


def shares(amount, total, reach, skew, full):
    loads = [(1 << 20) // math.isqrt(grade ** skew) + 1 for grade in range(1, amount + 1)]
    largest = reach if full else min(reach, max(-(-total // amount), total * loads[0] // sum(loads)))
    least = 1 if total - largest >= amount - 1 else 0
    holding, surplus = [largest] + [least] * (amount - 1), total - largest - least * (amount - 1)
    while surplus > 0:
        candidates = [i for i in range(1, amount) if holding[i] < largest] or [i for i in range(1, amount) if holding[i] < reach]
        mass, budget = sum([loads[i] for i in candidates]), surplus
        for i in candidates:
            extra = min(reach - holding[i], max(1, budget * loads[i] // mass), surplus)
            holding[i] = holding[i] + extra
            surplus = surplus - extra
    return np.array(holding)


def normal_values(own_key, extent, deviation, bound, cuts=(), kind=jnp.bfloat16):
    entries = jax.random.normal(own_key, extent, jnp.float32) * deviation
    if len(cuts) > 0:
        entries = block_levels(own_key, extent, cuts, -0.22, 0.18) * entries
    return jnp.clip(entries, min=-bound, max=bound).astype(kind)


def setup_inputs(seed: int = 0) -> dict:
    arg_keys = jax.random.split(jax.random.key(seed), 10)
    dna_embed = draw_dna_embed(jax.random.fold_in(arg_keys[9], 71), 0)
    site_owner_keys = jax.random.split(jax.random.fold_in(arg_keys[1], 1), HAPS * SEQ // L_DEV)
    site_owner_turns = jax.random.permutation(jax.random.fold_in(arg_keys[1], 3), HAPS * SEQ // L_DEV)
    site_owner = jax.vmap(lambda own, number: routed_block(jax.random.fold_in(arg_keys[1], 2), own, number, L_DEV, N_SEQ, 1, CAP, 2))(site_owner_keys, site_owner_turns).reshape((HAPS, SEQ, 1))
    site_row = with_ends(jax.random.randint(arg_keys[2], (HAPS, SEQ), 0, SITES_DEV), jax.random.fold_in(arg_keys[2], 1), 0, SITES_DEV - 1).astype(jnp.int32)
    variant_table = normal_values(arg_keys[3], (SITES, D), 1.0, 6.0, ((0, 16),))
    norm_gain = jnp.clip(1.0 + 0.18 * jax.random.normal(arg_keys[4], (D,), jnp.float32), 0.1, 1.9)
    conv_weight = normal_values(arg_keys[5], (CONV, D), 0.4, 2.390625)
    qkv_weight = draw_qkv_weight(jax.random.fold_in(arg_keys[9], 71), 0)
    out_weight = normal_values(arg_keys[7], (D, D), D ** -0.5, 0.1875, ((1, 2),))
    attn_gain = jnp.clip(1.0 + 0.18 * jax.random.normal(arg_keys[8], (D,), jnp.float32), 0.1, 1.9)
    return dict(dna_embed=dna_embed, site_owner=site_owner, site_row=site_row, variant_table=variant_table, norm_gain=norm_gain, conv_weight=conv_weight, qkv_weight=qkv_weight, out_weight=out_weight, attn_gain=attn_gain)


EPSILON = 1e-05

def rms_scale(values, gain):
    return values * lax.rsqrt(lax.optimization_barrier(jnp.mean(values * values, axis=-1, keepdims=True)) + EPSILON) * gain

def window_block(query, key_value, block_index):
    start = (block_index * L_DEV).astype(jnp.int32)
    q_block = lax.dynamic_slice_in_dim(query, start, L_DEV, 0)
    k_block = lax.dynamic_slice_in_dim(key_value, start, WINDOW + L_DEV, 0)
    q_where = start + jnp.arange(L_DEV, dtype=jnp.int32)
    k_where = start - WINDOW + jnp.arange(WINDOW + L_DEV, dtype=jnp.int32)
    allowed = (k_where[None, :] <= q_where[:, None]) & (k_where[None, :] > q_where[:, None] - WINDOW) & (k_where[None, :] >= 0)
    q_heads = q_block.reshape(L_DEV, HEADS, HEAD).astype(jnp.float32)
    k_heads = k_block[:, :D].reshape(WINDOW + L_DEV, HEADS, HEAD).astype(jnp.float32)
    v_heads = k_block[:, D:].reshape(WINDOW + L_DEV, HEADS, HEAD).astype(jnp.float32)
    scores = jnp.einsum('qhd,khd->hqk', q_heads, k_heads) * HEAD ** (-0.5)
    scores = jnp.where(allowed[None, :, :], scores, -jnp.inf)
    highest = lax.optimization_barrier(jnp.max(scores, axis=-1, keepdims=True))
    expo = jnp.exp(scores - highest)
    probs = (expo / lax.optimization_barrier(jnp.sum(expo, axis=-1, keepdims=True))).astype(jnp.bfloat16)
    attended = jnp.einsum('hqk,khd->qhd', probs.astype(jnp.float32), v_heads)
    return attended.reshape(L_DEV, D)

def one_haplotype(tokens_in, owner_ids, row_ids, variant_table, norm_gain, conv_weight, qkv_weight, out_weight, attn_gain):
    site_embed = variant_table[owner_ids * SITES_DEV + row_ids]
    resid = tokens_in.astype(jnp.float32) + site_embed.astype(jnp.float32)
    normed = rms_scale(resid, norm_gain).astype(jnp.bfloat16)
    padded = jnp.pad(normed, ((CONV - 1, 0), (0, 0)))
    conv_sum = jnp.zeros((SEQ, D), jnp.float32)
    for tap in range(CONV):
        conv_sum = conv_sum + conv_weight[tap].astype(jnp.float32) * padded[CONV - 1 - tap:CONV - 1 - tap + SEQ].astype(jnp.float32)
    conv_out = conv_sum.astype(jnp.bfloat16)
    qkv = jnp.dot(conv_out, qkv_weight, preferred_element_type=jnp.float32).astype(jnp.bfloat16)
    query = qkv[:, :D]
    key_value = jnp.pad(qkv[:, D:], ((WINDOW, 0), (0, 0)))
    blocks = lax.map(lambda index: window_block(query, key_value, index), jnp.arange(SEQ // L_DEV, dtype=jnp.int32))
    attended = blocks.reshape(SEQ, D)
    attn_normed = rms_scale(attended, attn_gain).astype(jnp.bfloat16)
    return jnp.dot(attn_normed, out_weight, preferred_element_type=jnp.float32).astype(jnp.bfloat16)

def reference(dna_embed, site_owner, site_row, variant_table, norm_gain, conv_weight, qkv_weight, out_weight, attn_gain):
    results = []
    for haplotype in range(HAPS):
        results.append(one_haplotype(dna_embed[haplotype], site_owner[haplotype, :, 0], site_row[haplotype], variant_table, norm_gain, conv_weight, qkv_weight, out_weight, attn_gain))
    return jnp.stack(results, axis=0)
```

```python
import functools

import jax
import jax.numpy as jnp
from jax import lax
from jax.experimental import pallas as pl
from jax.experimental.pallas import tpu as pltpu
from jax.sharding import PartitionSpec as P

HEAD = 64
WINDOW = 2048


EPSILON = 1e-05


def shifted(value, axis, steps):
    count = lax.axis_size(axis)
    first, last = (max(0, -steps), min(count, count - steps))
    return lax.ppermute(value, axis, [(source, source + steps) for source in range(first, last)])


def rms_scale(values, gain):
    return values * lax.rsqrt(jnp.mean(values * values, axis=-1, keepdims=True) + EPSILON) * gain


def local(
    dna_embed,
    site_owner,
    site_row,
    variant_table,
    norm_gain,
    conv_weight,
    qkv_weight,
    out_weight,
    attn_gain,
):
    seq_rank = lax.axis_index("seq")
    seq_count = lax.axis_size("seq")
    tok_rows = dna_embed.shape[1]
    model_width = dna_embed.shape[2]
    slot_count = max(2, 2 * tok_rows // seq_count)
    owner_ids = site_owner[0, :, 0]
    wanted_rows = site_row[0]
    owner_onehot = (owner_ids[:, None] == jnp.arange(seq_count, dtype=jnp.int32)[None, :]).astype(
        jnp.int32
    )
    earlier_same = jnp.cumsum(owner_onehot, axis=0) - owner_onehot
    rank_within = jnp.sum(earlier_same * owner_onehot, axis=1)
    slot_index = owner_ids * slot_count + rank_within
    request_table = jnp.zeros((seq_count * slot_count,), jnp.int32).at[slot_index].set(wanted_rows)
    request_table = request_table.reshape(seq_count, slot_count)
    found = variant_table[
        lax.all_to_all(request_table, "seq", split_axis=0, concat_axis=0, tiled=True)
    ]
    fetched = lax.all_to_all(found, "seq", split_axis=0, concat_axis=0, tiled=True)
    site_embed = fetched.reshape(seq_count * slot_count, model_width)[slot_index]
    resid = dna_embed[0].astype(jnp.float32) + site_embed.astype(jnp.float32)
    normed = rms_scale(resid, norm_gain).astype(jnp.bfloat16)
    taps = conv_weight.shape[0]
    rim_rows = shifted(normed[tok_rows - (taps - 1) :], "seq", 1)
    padded = jnp.concatenate([rim_rows, normed], axis=0)
    conv_sum = jnp.zeros((tok_rows, model_width), jnp.float32)
    for tap in range(taps):
        conv_sum = conv_sum + conv_weight[tap].astype(jnp.float32) * padded[
            taps - 1 - tap : taps - 1 - tap + tok_rows
        ].astype(jnp.float32)
    conv_out = conv_sum.astype(jnp.bfloat16)
    full_qkv, full_out = (
        lax.all_gather(qkv_weight, "fsdp", axis=1, tiled=True),
        lax.all_gather(out_weight, "fsdp", axis=1, tiled=True),
    )
    qkv = jnp.dot(conv_out, full_qkv, preferred_element_type=jnp.float32).astype(jnp.bfloat16)
    reach_count = WINDOW // tok_rows
    earlier = [shifted(conv_out, "seq", reach_count - offset) for offset in range(reach_count)]
    past_conv = jnp.concatenate(earlier, axis=0)
    past_kv = jnp.dot(
        past_conv, full_qkv[:, model_width:], preferred_element_type=jnp.float32
    ).astype(jnp.bfloat16)
    return attention(qkv, past_kv, full_out, attn_gain[None, :], tok_rows, model_width)[None, :, :]


def attention_kernel(tok_rows, q_ref, kp_ref, vp_ref, kl_ref, vl_ref, out_w_ref, gain_ref, o_ref, att_ref):
    pair = pl.program_id(0)
    pairs = pl.num_programs(0)
    rank = lax.axis_index("seq")
    past = kp_ref.shape[0]
    lanes = q_ref.shape[1]
    low_half = lax.broadcasted_iota(jnp.int32, (tok_rows, lanes), 1) < HEAD
    row = lax.broadcasted_iota(jnp.int32, (tok_rows, tok_rows), 0)
    col = lax.broadcasted_iota(jnp.int32, (tok_rows, tok_rows), 1)
    recent = col <= row
    absent = past - rank * tok_rows
    mid_col = tok_rows + lax.broadcasted_iota(jnp.int32, (tok_rows, past - tok_rows), 1)
    query = q_ref[...]
    scaled = query * jnp.asarray(HEAD ** (-0.5), query.dtype)
    nt = (((1,), (1,)), ((), ()))
    halves = []
    for half in range(2):
        keep = low_half if half == 0 else jnp.logical_not(low_half)
        q_head = jnp.where(keep, scaled, jnp.zeros_like(scaled))
        s_mid = lax.dot_general(q_head, kp_ref[tok_rows:, :], nt, preferred_element_type=jnp.float32)
        s_old = lax.dot_general(q_head, kp_ref[:tok_rows, :], nt, preferred_element_type=jnp.float32)
        s_new = lax.dot_general(q_head, kl_ref[...], nt, preferred_element_type=jnp.float32)
        s_mid = jnp.where(mid_col >= absent, s_mid, -jnp.inf)
        s_old = jnp.where(col >= absent, s_old, -jnp.inf)
        s_edge = jnp.where(recent, s_new, s_old)
        highest = jnp.maximum(
            jnp.max(s_mid, axis=-1, keepdims=True), jnp.max(s_edge, axis=-1, keepdims=True)
        )
        e_mid = jnp.exp(s_mid - highest)
        e_edge = jnp.exp(s_edge - highest)
        total = jnp.sum(e_mid, axis=-1, keepdims=True) + jnp.sum(e_edge, axis=-1, keepdims=True)
        inverse = 1.0 / total
        p_mid = (e_mid * inverse).astype(jnp.bfloat16)
        p_edge = e_edge * inverse
        p_new = jnp.where(recent, p_edge, 0.0).astype(jnp.bfloat16)
        p_old = jnp.where(recent, 0.0, p_edge).astype(jnp.bfloat16)
        halves.append(
            jnp.dot(p_mid, vp_ref[tok_rows:, :], preferred_element_type=jnp.float32)
            + jnp.dot(p_old, vp_ref[:tok_rows, :], preferred_element_type=jnp.float32)
            + jnp.dot(p_new, vl_ref[...], preferred_element_type=jnp.float32)
        )
    att_ref[:, pl.ds(pl.multiple_of(pair * lanes, lanes), lanes)] = jnp.where(
        low_half, halves[0], halves[1]
    )

    @pl.when(pair == pairs - 1)
    def _():
        attended = att_ref[...]
        normed = rms_scale(attended, gain_ref[...]).astype(jnp.bfloat16)
        o_ref[...] = jnp.dot(
            normed, out_w_ref[...], preferred_element_type=jnp.float32
        ).astype(o_ref.dtype)


def attention(qkv, past_kv, out_weight, gain, tok_rows, model_width):
    lanes = 2 * HEAD
    pairs = model_width // lanes
    past = past_kv.shape[0]
    return pl.pallas_call(
        functools.partial(attention_kernel, tok_rows),
        grid=(pairs,),
        out_shape=jax.ShapeDtypeStruct((tok_rows, model_width), jnp.bfloat16),
        in_specs=[
            pl.BlockSpec((tok_rows, lanes), lambda h: (0, h)),
            pl.BlockSpec((past, lanes), lambda h: (0, h)),
            pl.BlockSpec((past, lanes), lambda h: (0, pairs + h)),
            pl.BlockSpec((tok_rows, lanes), lambda h: (0, pairs + h)),
            pl.BlockSpec((tok_rows, lanes), lambda h: (0, 2 * pairs + h)),
            pl.BlockSpec(out_weight.shape, lambda h: (0, 0)),
            pl.BlockSpec(gain.shape, lambda h: (0, 0)),
        ],
        out_specs=pl.BlockSpec((tok_rows, model_width), lambda h: (0, 0)),
        scratch_shapes=[pltpu.VMEM((tok_rows, model_width), jnp.float32)],
        compiler_params=pltpu.CompilerParams(vmem_limit_bytes=48 * 1024 * 1024),
        cost_estimate=pl.CostEstimate(
            flops=8 * tok_rows * (past + tok_rows) * model_width,
            bytes_accessed=4 * past * model_width,
            transcendentals=tok_rows * past * model_width // HEAD,
        ),
        name="window_attention",
    )(qkv, past_kv, past_kv, qkv, qkv, out_weight, gain)


def solution(mesh):
    in_specs = (
        P("fsdp", "seq", None),
        P("fsdp", "seq", None),
        P("fsdp", "seq"),
        P("seq", None),
        P(),
        P(),
        P(None, "fsdp"),
        P(None, "fsdp"),
        P(),
    )
    out_specs = P("fsdp", "seq", None)
    return jax.shard_map(local, mesh=mesh, in_specs=in_specs, out_specs=out_specs, check_vma=False)
```

```python
import functools

import jax
import jax.numpy as jnp
from jax import lax
from jax.experimental import pallas as pl
from jax.experimental.pallas import tpu as pltpu
from jax.sharding import PartitionSpec as P

HEAD = 64
WINDOW = 2048


EPSILON = 1e-05


def shifted(value, axis, steps):
    count = lax.axis_size(axis)
    first, last = (max(0, -steps), min(count, count - steps))
    return lax.ppermute(value, axis, [(source, source + steps) for source in range(first, last)])


def rms_scale(values, gain):
    return values * lax.rsqrt(jnp.mean(values * values, axis=-1, keepdims=True) + EPSILON) * gain


def local(
    dna_embed,
    site_owner,
    site_row,
    variant_table,
    norm_gain,
    conv_weight,
    qkv_weight,
    out_weight,
    attn_gain,
):
    seq_rank = lax.axis_index("seq")
    seq_count = lax.axis_size("seq")
    tok_rows = dna_embed.shape[1]
    model_width = dna_embed.shape[2]
    slot_count = max(2, 2 * tok_rows // seq_count)
    owner_ids = site_owner[0, :, 0]
    wanted_rows = site_row[0]
    owner_onehot = (owner_ids[:, None] == jnp.arange(seq_count, dtype=jnp.int32)[None, :]).astype(
        jnp.int32
    )
    earlier_same = jnp.cumsum(owner_onehot, axis=0) - owner_onehot
    rank_within = jnp.sum(earlier_same * owner_onehot, axis=1)
    slot_index = owner_ids * slot_count + rank_within
    request_table = jnp.zeros((seq_count * slot_count,), jnp.int32).at[slot_index].set(wanted_rows)
    request_table = request_table.reshape(seq_count, slot_count)
    found = variant_table[
        lax.all_to_all(request_table, "seq", split_axis=0, concat_axis=0, tiled=True)
    ]
    fetched = lax.all_to_all(found, "seq", split_axis=0, concat_axis=0, tiled=True)
    site_embed = fetched.reshape(seq_count * slot_count, model_width)[slot_index]
    resid = dna_embed[0].astype(jnp.float32) + site_embed.astype(jnp.float32)
    normed = rms_scale(resid, norm_gain).astype(jnp.bfloat16)
    taps = conv_weight.shape[0]
    rim_rows = shifted(normed[tok_rows - (taps - 1) :], "seq", 1)
    padded = jnp.concatenate([rim_rows, normed], axis=0)
    conv_sum = jnp.zeros((tok_rows, model_width), jnp.float32)
    for tap in range(taps):
        conv_sum = conv_sum + conv_weight[tap].astype(jnp.float32) * padded[
            taps - 1 - tap : taps - 1 - tap + tok_rows
        ].astype(jnp.float32)
    conv_out = conv_sum.astype(jnp.bfloat16)
    full_qkv, full_out = (
        lax.all_gather(qkv_weight, "fsdp", axis=1, tiled=True),
        lax.all_gather(out_weight, "fsdp", axis=1, tiled=True),
    )
    window = gather_window(conv_out)
    query = jnp.dot(
        conv_out, full_qkv[:, :model_width], preferred_element_type=jnp.float32
    ).astype(jnp.bfloat16)
    key_value = jnp.dot(
        window, full_qkv[:, model_width:], preferred_element_type=jnp.float32
    ).astype(jnp.bfloat16)
    return attention(query, key_value, full_out, attn_gain[None, :], tok_rows, model_width)[None, :, :]


MESH = pl.DeviceIdType.MESH
CHUNKS = 4
REACH_CHIPS = 4


def window_kernel(count, conv_ref, win_ref, send_sem, recv_sem):
    me = lax.axis_index("seq")
    rows = conv_ref.shape[0]
    part = rows // CHUNKS
    core = lax.rem(me, 2)
    odd = lax.rem(me // 2, 2)
    ahead = lax.rem(me + 4, count)
    behind = lax.rem(me + count - 4, count)
    beside = me + 2 - 4 * odd
    twin = me + 1 - 2 * core

    def slot(back, chunk):
        first = ((REACH_CHIPS - back) * 2 + core) * rows + chunk * part
        return win_ref.at[pl.ds(pl.multiple_of(first, part), part)]

    own = pl.multiple_of((REACH_CHIPS * 2 + core) * rows, rows)
    win_ref[pl.ds(own, rows), :] = conv_ref[...]

    barrier = pltpu.get_barrier_semaphore()
    for other in (ahead, behind, beside, twin):
        pl.semaphore_signal(barrier, inc=1, device_id={"seq": other}, device_id_type=MESH)
    pl.semaphore_wait(barrier, 4)

    def message(kind, chunk, source_back, target_back, target):
        return pltpu.make_async_remote_copy(
            src_ref=slot(source_back, chunk),
            dst_ref=slot(target_back, chunk),
            send_sem=send_sem.at[kind, chunk],
            recv_sem=recv_sem.at[kind, chunk],
            device_id={"seq": target},
            device_id_type=MESH,
        )

    chunks = range(CHUNKS)
    two = [message(0, j, 0, 2, ahead) for j in chunks]
    four = [message(1, j, 2, 4, ahead) for j in chunks]
    one = [message(2, j, 2 * odd, 1, beside) for j in chunks]
    three = [message(3, j, 2 + 2 * odd, 3, beside) for j in chunks]
    share = [[message(4 + back, j, back, back, twin) for j in chunks] for back in range(5)]
    for j in chunks:
        two[j].start()
    for j in chunks:
        share[0][j].start()
    for j in chunks:
        two[j].wait_recv()
        four[j].start()
        one[j].start()
        share[2][j].start()
    for j in chunks:
        four[j].wait_recv()
        three[j].start()
        share[4][j].start()
        one[j].wait_recv()
        share[1][j].start()
    for j in chunks:
        three[j].wait_recv()
        share[3][j].start()
    for back in range(5):
        for j in chunks:
            share[back][j].wait_recv()
    for group in [two, four, one, three] + share:
        for j in chunks:
            group[j].wait_send()


def gather_window(conv_out):
    count = lax.axis_size("seq")
    rows, width = conv_out.shape
    slots = 2 * REACH_CHIPS + 2
    return pl.pallas_call(
        functools.partial(window_kernel, count),
        out_shape=jax.ShapeDtypeStruct((slots * rows, width), conv_out.dtype),
        in_specs=[pl.BlockSpec(memory_space=pltpu.VMEM)],
        out_specs=pl.BlockSpec(memory_space=pltpu.VMEM),
        scratch_shapes=[
            pltpu.SemaphoreType.DMA((9, CHUNKS)),
            pltpu.SemaphoreType.DMA((9, CHUNKS)),
        ],
        compiler_params=pltpu.CompilerParams(
            collective_id=1, has_side_effects=True, vmem_limit_bytes=48 * 1024 * 1024
        ),
        cost_estimate=pl.CostEstimate(
            flops=0, bytes_accessed=2 * slots * rows * width, transcendentals=0
        ),
        name="gather_window",
    )(conv_out)


def attention_kernel(tok_rows, q_ref, k_ref, v_ref, out_w_ref, gain_ref, o_ref, att_ref):
    pair = pl.program_id(0)
    pairs = pl.num_programs(0)
    rank = lax.axis_index("seq")
    past = 2 * REACH_CHIPS * tok_rows
    shift = pl.multiple_of(lax.rem(rank, 2) * tok_rows, tok_rows)
    old = pl.ds(shift, tok_rows)
    mid = pl.ds(pl.multiple_of(shift + tok_rows, tok_rows), past - tok_rows)
    new = pl.ds(pl.multiple_of(shift + past, tok_rows), tok_rows)
    lanes = q_ref.shape[1]
    low_half = lax.broadcasted_iota(jnp.int32, (tok_rows, lanes), 1) < HEAD
    row = lax.broadcasted_iota(jnp.int32, (tok_rows, tok_rows), 0)
    col = lax.broadcasted_iota(jnp.int32, (tok_rows, tok_rows), 1)
    recent = col <= row
    absent = past - rank * tok_rows
    mid_col = tok_rows + lax.broadcasted_iota(jnp.int32, (tok_rows, past - tok_rows), 1)
    query = q_ref[...]
    scaled = query * jnp.asarray(HEAD ** (-0.5), query.dtype)
    nt = (((1,), (1,)), ((), ()))
    halves = []
    for half in range(2):
        keep = low_half if half == 0 else jnp.logical_not(low_half)
        q_head = jnp.where(keep, scaled, jnp.zeros_like(scaled))
        s_mid = lax.dot_general(q_head, k_ref[mid, :], nt, preferred_element_type=jnp.float32)
        s_old = lax.dot_general(q_head, k_ref[old, :], nt, preferred_element_type=jnp.float32)
        s_new = lax.dot_general(q_head, k_ref[new, :], nt, preferred_element_type=jnp.float32)
        s_mid = jnp.where(mid_col >= absent, s_mid, -jnp.inf)
        s_old = jnp.where(col >= absent, s_old, -jnp.inf)
        s_edge = jnp.where(recent, s_new, s_old)
        highest = jnp.maximum(
            jnp.max(s_mid, axis=-1, keepdims=True), jnp.max(s_edge, axis=-1, keepdims=True)
        )
        e_mid = jnp.exp(s_mid - highest)
        e_edge = jnp.exp(s_edge - highest)
        total = jnp.sum(e_mid, axis=-1, keepdims=True) + jnp.sum(e_edge, axis=-1, keepdims=True)
        inverse = 1.0 / total
        p_mid = (e_mid * inverse).astype(jnp.bfloat16)
        p_edge = e_edge * inverse
        p_new = jnp.where(recent, p_edge, 0.0).astype(jnp.bfloat16)
        p_old = jnp.where(recent, 0.0, p_edge).astype(jnp.bfloat16)
        halves.append(
            jnp.dot(p_mid, v_ref[mid, :], preferred_element_type=jnp.float32)
            + jnp.dot(p_old, v_ref[old, :], preferred_element_type=jnp.float32)
            + jnp.dot(p_new, v_ref[new, :], preferred_element_type=jnp.float32)
        )
    att_ref[:, pl.ds(pl.multiple_of(pair * lanes, lanes), lanes)] = jnp.where(
        low_half, halves[0], halves[1]
    )

    @pl.when(pair == pairs - 1)
    def _():
        attended = att_ref[...]
        normed = rms_scale(attended, gain_ref[...]).astype(jnp.bfloat16)
        o_ref[...] = jnp.dot(
            normed, out_w_ref[...], preferred_element_type=jnp.float32
        ).astype(o_ref.dtype)


def attention(query, key_value, out_weight, gain, tok_rows, model_width):
    lanes = 2 * HEAD
    pairs = model_width // lanes
    span = key_value.shape[0]
    past = 2 * REACH_CHIPS * tok_rows
    return pl.pallas_call(
        functools.partial(attention_kernel, tok_rows),
        grid=(pairs,),
        out_shape=jax.ShapeDtypeStruct((tok_rows, model_width), jnp.bfloat16),
        in_specs=[
            pl.BlockSpec((tok_rows, lanes), lambda h: (0, h)),
            pl.BlockSpec((span, lanes), lambda h: (0, h)),
            pl.BlockSpec((span, lanes), lambda h: (0, pairs + h)),
            pl.BlockSpec(out_weight.shape, lambda h: (0, 0)),
            pl.BlockSpec(gain.shape, lambda h: (0, 0)),
        ],
        out_specs=pl.BlockSpec((tok_rows, model_width), lambda h: (0, 0)),
        scratch_shapes=[pltpu.VMEM((tok_rows, model_width), jnp.float32)],
        compiler_params=pltpu.CompilerParams(vmem_limit_bytes=48 * 1024 * 1024),
        cost_estimate=pl.CostEstimate(
            flops=8 * tok_rows * (past + tok_rows) * model_width,
            bytes_accessed=4 * past * model_width,
            transcendentals=tok_rows * past * model_width // HEAD,
        ),
        name="window_attention",
    )(query, key_value, key_value, out_weight, gain)


def solution(mesh):
    in_specs = (
        P("fsdp", "seq", None),
        P("fsdp", "seq", None),
        P("fsdp", "seq"),
        P("seq", None),
        P(),
        P(),
        P(None, "fsdp"),
        P(None, "fsdp"),
        P(),
    )
    out_specs = P("fsdp", "seq", None)
    return jax.shard_map(local, mesh=mesh, in_specs=in_specs, out_specs=out_specs, check_vma=False)
```

```python
import functools

import jax
import jax.numpy as jnp
from jax import lax
from jax.experimental import pallas as pl
from jax.experimental.pallas import tpu as pltpu
from jax.sharding import PartitionSpec as P

HEAD = 64
WINDOW = 2048


EPSILON = 1e-05


def rms_scale(values, gain):
    return values * lax.rsqrt(jnp.mean(values * values, axis=-1, keepdims=True) + EPSILON) * gain


def local(
    dna_embed,
    site_owner,
    site_row,
    variant_table,
    norm_gain,
    conv_weight,
    qkv_weight,
    out_weight,
    attn_gain,
):
    seq_count = lax.axis_size("seq")
    tok_rows = dna_embed.shape[1]
    model_width = dna_embed.shape[2]
    slot_count = max(16, 2 * tok_rows // seq_count)
    owner_ids = site_owner[0, :, 0]
    wanted_rows = site_row[0]
    owner_onehot = (owner_ids[:, None] == jnp.arange(seq_count, dtype=jnp.int32)[None, :]).astype(
        jnp.int32
    )
    earlier_same = jnp.cumsum(owner_onehot, axis=0) - owner_onehot
    rank_within = jnp.sum(earlier_same * owner_onehot, axis=1)
    slot_index = owner_ids * slot_count + rank_within
    request_table = jnp.zeros((seq_count * slot_count,), jnp.int32).at[slot_index].set(wanted_rows)
    conv_out, full_qkv = embed_and_conv(
        jnp.broadcast_to(request_table[:, None], (seq_count * slot_count, LANES)),
        slot_index[:, None],
        dna_embed[0],
        variant_table,
        norm_gain[None, :],
        conv_weight,
        qkv_weight,
        slot_count,
    )
    window, full_out = gather_window(conv_out, out_weight)
    query = jnp.dot(
        conv_out, full_qkv[:, :model_width], preferred_element_type=jnp.float32
    ).astype(jnp.bfloat16)
    key_value = jnp.dot(
        window, full_qkv[:, model_width:], preferred_element_type=jnp.float32
    ).astype(jnp.bfloat16)
    return attention(query, key_value, full_out, attn_gain[None, :], tok_rows, model_width)[None, :, :]


MESH = pl.DeviceIdType.MESH
CHUNKS = 4
REACH_CHIPS = 4


def window_kernel(
    count, conv_ref, shard_ref, win_ref, full_ref, send_sem, recv_sem, swap_sem, local_sem
):
    me = lax.axis_index("seq")
    rows = conv_ref.shape[0]
    part = rows // CHUNKS
    core = lax.rem(me, 2)
    odd = lax.rem(me // 2, 2)
    ahead = lax.rem(me + 4, count)
    behind = lax.rem(me + count - 4, count)
    beside = me + 2 - 4 * odd
    twin = me + 1 - 2 * core

    def slot(back, chunk):
        first = ((REACH_CHIPS - back) * 2 + core) * rows + chunk * part
        return win_ref.at[pl.ds(pl.multiple_of(first, part), part)]

    own = pl.multiple_of((REACH_CHIPS * 2 + core) * rows, rows)
    win_ref[pl.ds(own, rows), :] = conv_ref[...]

    barrier = pltpu.get_barrier_semaphore()
    for other in (ahead, behind, beside, twin):
        pl.semaphore_signal(barrier, inc=1, device_id={"seq": other}, device_id_type=MESH)
    pl.semaphore_signal(
        barrier, inc=1, device_id={"fsdp": 1 - lax.axis_index("fsdp")}, device_id_type=MESH
    )
    pl.semaphore_wait(barrier, 5)
    swap = WeightSwap(shard_ref, full_ref, swap_sem, local_sem, 1)
    swap.start()

    def message(kind, chunk, source_back, target_back, target):
        return pltpu.make_async_remote_copy(
            src_ref=slot(source_back, chunk),
            dst_ref=slot(target_back, chunk),
            send_sem=send_sem.at[kind, chunk],
            recv_sem=recv_sem.at[kind, chunk],
            device_id={"seq": target},
            device_id_type=MESH,
        )

    chunks = range(CHUNKS)
    two = [message(0, j, 0, 2, ahead) for j in chunks]
    four = [message(1, j, 2, 4, ahead) for j in chunks]
    one = [message(2, j, 2 * odd, 1, beside) for j in chunks]
    three = [message(3, j, 2 + 2 * odd, 3, beside) for j in chunks]
    share = [[message(4 + back, j, back, back, twin) for j in chunks] for back in range(5)]
    for j in chunks:
        two[j].start()
    for j in chunks:
        share[0][j].start()
    for j in chunks:
        two[j].wait_recv()
        four[j].start()
        one[j].start()
        share[2][j].start()
    for j in chunks:
        four[j].wait_recv()
        three[j].start()
        share[4][j].start()
        one[j].wait_recv()
        share[1][j].start()
    for j in chunks:
        three[j].wait_recv()
        share[3][j].start()
    for back in range(5):
        for j in chunks:
            share[back][j].wait_recv()
    for group in [two, four, one, three] + share:
        for j in chunks:
            group[j].wait_send()
    swap.finish()


def gather_window(conv_out, shard):
    count = lax.axis_size("seq")
    rows, width = conv_out.shape
    slots = 2 * REACH_CHIPS + 2
    return pl.pallas_call(
        functools.partial(window_kernel, count),
        out_shape=[
            jax.ShapeDtypeStruct((slots * rows, width), conv_out.dtype),
            jax.ShapeDtypeStruct((shard.shape[0], 2 * shard.shape[1]), shard.dtype),
        ],
        in_specs=[pl.BlockSpec(memory_space=pltpu.VMEM), pl.BlockSpec(memory_space=pl.ANY)],
        out_specs=[pl.BlockSpec(memory_space=pltpu.VMEM), pl.BlockSpec(memory_space=pl.ANY)],
        scratch_shapes=[
            pltpu.SemaphoreType.DMA((9, CHUNKS)),
            pltpu.SemaphoreType.DMA((9, CHUNKS)),
            pltpu.SemaphoreType.DMA((4, 1)),
            pltpu.SemaphoreType.DMA,
        ],
        compiler_params=pltpu.CompilerParams(
            collective_id=1, has_side_effects=True, vmem_limit_bytes=48 * 1024 * 1024
        ),
        cost_estimate=pl.CostEstimate(
            flops=0, bytes_accessed=2 * slots * rows * width, transcendentals=0
        ),
        name="gather_window",
    )(conv_out, shard)


LANES = 128
EDGE = 16


class WeightSwap:
    def __init__(self, shard_ref, full_ref, sems, local_sem, parts):
        me = lax.axis_index("seq")
        half = lax.axis_index("fsdp")
        core = lax.rem(me, 2)
        rows, cols = shard_ref.shape
        part = rows // 2 // parts

        def block(ref, chunk, column):
            first = pl.multiple_of(core * (rows // 2) + chunk * part, part)
            return ref.at[pl.ds(first, part), pl.ds(pl.multiple_of(column * cols, LANES), cols)]

        self.own = pltpu.make_async_copy(
            shard_ref, full_ref.at[:, pl.ds(pl.multiple_of(half * cols, LANES), cols)], local_sem
        )
        self.across = [
            pltpu.make_async_remote_copy(
                src_ref=block(shard_ref, j, 0),
                dst_ref=block(full_ref, j, half),
                send_sem=sems.at[0, j],
                recv_sem=sems.at[1, j],
                device_id={"fsdp": 1 - half},
                device_id_type=MESH,
            )
            for j in range(parts)
        ]
        self.pass_on = [
            pltpu.make_async_remote_copy(
                src_ref=block(full_ref, j, 1 - half),
                dst_ref=block(full_ref, j, 1 - half),
                send_sem=sems.at[2, j],
                recv_sem=sems.at[3, j],
                device_id={"seq": me + 1 - 2 * core},
                device_id_type=MESH,
            )
            for j in range(parts)
        ]

    def start(self):
        for copy in self.across:
            copy.start()
        self.own.start()

    def finish(self):
        for arrive, give in zip(self.across, self.pass_on):
            arrive.wait_recv()
            give.start()
        self.own.wait()
        for arrive, give in zip(self.across, self.pass_on):
            arrive.wait_send()
            give.wait()


def embed_kernel(
    count, slots, request_ref, slot_ref, dna_ref, table_ref, gain_ref, taps_ref, shard_ref,
    conv_ref, full_ref,
    inbox, found, fetched, edge_out, edge_in,
    ask_send, ask_recv, give_send, give_recv, edge_sem, swap_sem, local_sem,
):
    me = lax.axis_index("seq")
    rows = dna_ref.shape[0]
    site_rows = table_ref.shape[0]
    batch = LANES // slots

    def at(ref, index):
        return ref.at[pl.ds(pl.multiple_of(index * slots, slots), slots)]

    def ask(step):
        target = lax.rem(me + step, count)
        return pltpu.make_async_remote_copy(
            src_ref=at(request_ref, target),
            dst_ref=at(inbox, step),
            send_sem=ask_send.at[step],
            recv_sem=ask_recv.at[step],
            device_id={"seq": target},
            device_id_type=MESH,
        )

    def give(step):
        return pltpu.make_async_remote_copy(
            src_ref=at(found, step),
            dst_ref=at(fetched, me),
            send_sem=give_send.at[step],
            recv_sem=give_recv.at[step],
            device_id={"seq": lax.rem(me + count - step, count)},
            device_id_type=MESH,
        )

    swap = WeightSwap(shard_ref, full_ref, swap_sem, local_sem, 2)
    barrier = pltpu.get_barrier_semaphore()

    def greet(step, carry):
        pl.semaphore_signal(
            barrier, inc=1, device_id={"seq": lax.rem(me + step, count)}, device_id_type=MESH
        )
        return carry

    lax.fori_loop(1, count, greet, 0)
    pl.semaphore_signal(
        barrier, inc=1, device_id={"fsdp": 1 - lax.axis_index("fsdp")}, device_id_type=MESH
    )
    pl.semaphore_wait(barrier, count)

    def each(first, action):
        def body(step, carry):
            action(step)
            return carry

        lax.fori_loop(first, count, body, 0)

    each(1, lambda step: ask(step).start())
    swap.start()
    inbox[0:slots, :] = request_ref[pl.ds(pl.multiple_of(me * slots, slots), slots), :]
    lane = lax.broadcasted_iota(jnp.int32, (LANES, LANES), 1)
    for group in range(count // batch):
        steps = range(group * batch, (group + 1) * batch)
        for step in steps:
            if step > 0:
                ask(step).wait_recv()
        ids = inbox[group * LANES : (group + 1) * LANES, :]
        pick = jnp.concatenate(
            [
                jnp.where(ids - base == lane, 1.0, 0.0).astype(jnp.bfloat16)
                for base in range(0, site_rows, LANES)
            ],
            axis=1,
        )
        got = jnp.dot(pick, table_ref[...], preferred_element_type=jnp.float32)
        found[group * LANES : (group + 1) * LANES, :] = got.astype(jnp.bfloat16)
        for step in steps:
            if step > 0:
                give(step).start()
    fetched[pl.ds(pl.multiple_of(me * slots, slots), slots), :] = found[0:slots, :]
    each(1, lambda step: give(step).wait_recv())

    place = lax.broadcasted_iota(jnp.int32, (rows, count * slots), 1)
    pick = jnp.where(slot_ref[...] == place, 1.0, 0.0).astype(jnp.bfloat16)
    site_embed = jnp.dot(pick, fetched[...], preferred_element_type=jnp.float32)
    resid = dna_ref[...].astype(jnp.float32) + site_embed
    normed = rms_scale(resid, gain_ref[...]).astype(jnp.bfloat16)
    edge_out[...] = normed[rows - EDGE :, :]
    edge = pltpu.make_async_remote_copy(
        src_ref=edge_out,
        dst_ref=edge_in,
        send_sem=edge_sem.at[0],
        recv_sem=edge_sem.at[1],
        device_id={"seq": lax.rem(me + 1, count)},
        device_id_type=MESH,
    )
    edge.start()
    edge.wait()
    before = jnp.where(me > 0, edge_in[...].astype(jnp.float32), 0.0)
    padded = jnp.concatenate([before, normed.astype(jnp.float32)], axis=0)
    total = jnp.zeros(dna_ref.shape, jnp.float32)
    for tap in range(taps_ref.shape[0]):
        total = total + taps_ref[tap : tap + 1, :].astype(jnp.float32) * padded[
            EDGE - tap : EDGE - tap + rows
        ]
    conv_ref[...] = total.astype(jnp.bfloat16)
    each(1, lambda step: ask(step).wait_send())
    each(1, lambda step: give(step).wait_send())
    swap.finish()


def embed_and_conv(requests, slot_index, dna, table, gain, taps, shard, slots):
    count = lax.axis_size("seq")
    rows, width = dna.shape
    vmem = pl.BlockSpec(memory_space=pltpu.VMEM)
    anywhere = pl.BlockSpec(memory_space=pl.ANY)
    dma = pltpu.SemaphoreType.DMA
    return pl.pallas_call(
        functools.partial(embed_kernel, count, slots),
        out_shape=[
            jax.ShapeDtypeStruct((rows, width), jnp.bfloat16),
            jax.ShapeDtypeStruct((shard.shape[0], 2 * shard.shape[1]), shard.dtype),
        ],
        in_specs=[vmem] * 6 + [anywhere],
        out_specs=[vmem, anywhere],
        scratch_shapes=[
            pltpu.VMEM((count * slots, LANES), jnp.int32),
            pltpu.VMEM((count * slots, width), jnp.bfloat16),
            pltpu.VMEM((count * slots, width), jnp.bfloat16),
            pltpu.VMEM((EDGE, width), jnp.bfloat16),
            pltpu.VMEM((EDGE, width), jnp.bfloat16),
            dma((count,)),
            dma((count,)),
            dma((count,)),
            dma((count,)),
            dma((2,)),
            dma((4, 2)),
            dma,
        ],
        compiler_params=pltpu.CompilerParams(
            collective_id=2, has_side_effects=True, vmem_limit_bytes=48 * 1024 * 1024
        ),
        cost_estimate=pl.CostEstimate(
            flops=4 * rows * table.size, bytes_accessed=2 * table.size, transcendentals=0
        ),
        name="embed_and_conv",
    )(requests, slot_index, dna, table, gain, taps, shard)


def attention_kernel(tok_rows, q_ref, k_ref, v_ref, out_w_ref, gain_ref, o_ref, att_ref):
    pair = pl.program_id(0)
    pairs = pl.num_programs(0)
    rank = lax.axis_index("seq")
    past = 2 * REACH_CHIPS * tok_rows
    shift = pl.multiple_of(lax.rem(rank, 2) * tok_rows, tok_rows)
    old = pl.ds(shift, tok_rows)
    mid = pl.ds(pl.multiple_of(shift + tok_rows, tok_rows), past - tok_rows)
    new = pl.ds(pl.multiple_of(shift + past, tok_rows), tok_rows)
    lanes = q_ref.shape[1]
    low_half = lax.broadcasted_iota(jnp.int32, (tok_rows, lanes), 1) < HEAD
    row = lax.broadcasted_iota(jnp.int32, (tok_rows, tok_rows), 0)
    col = lax.broadcasted_iota(jnp.int32, (tok_rows, tok_rows), 1)
    recent = col <= row
    absent = past - rank * tok_rows
    mid_col = tok_rows + lax.broadcasted_iota(jnp.int32, (tok_rows, past - tok_rows), 1)
    query = q_ref[...]
    scaled = query * jnp.asarray(HEAD ** (-0.5), query.dtype)
    nt = (((1,), (1,)), ((), ()))
    halves = []
    for half in range(2):
        keep = low_half if half == 0 else jnp.logical_not(low_half)
        q_head = jnp.where(keep, scaled, jnp.zeros_like(scaled))
        s_mid = lax.dot_general(q_head, k_ref[mid, :], nt, preferred_element_type=jnp.float32)
        s_old = lax.dot_general(q_head, k_ref[old, :], nt, preferred_element_type=jnp.float32)
        s_new = lax.dot_general(q_head, k_ref[new, :], nt, preferred_element_type=jnp.float32)
        s_mid = jnp.where(mid_col >= absent, s_mid, -jnp.inf)
        s_old = jnp.where(col >= absent, s_old, -jnp.inf)
        s_edge = jnp.where(recent, s_new, s_old)
        highest = jnp.maximum(
            jnp.max(s_mid, axis=-1, keepdims=True), jnp.max(s_edge, axis=-1, keepdims=True)
        )
        e_mid = jnp.exp(s_mid - highest)
        e_edge = jnp.exp(s_edge - highest)
        total = jnp.sum(e_mid, axis=-1, keepdims=True) + jnp.sum(e_edge, axis=-1, keepdims=True)
        inverse = 1.0 / total
        p_mid = (e_mid * inverse).astype(jnp.bfloat16)
        p_edge = e_edge * inverse
        p_new = jnp.where(recent, p_edge, 0.0).astype(jnp.bfloat16)
        p_old = jnp.where(recent, 0.0, p_edge).astype(jnp.bfloat16)
        halves.append(
            jnp.dot(p_mid, v_ref[mid, :], preferred_element_type=jnp.float32)
            + jnp.dot(p_old, v_ref[old, :], preferred_element_type=jnp.float32)
            + jnp.dot(p_new, v_ref[new, :], preferred_element_type=jnp.float32)
        )
    att_ref[:, pl.ds(pl.multiple_of(pair * lanes, lanes), lanes)] = jnp.where(
        low_half, halves[0], halves[1]
    )

    @pl.when(pair == pairs - 1)
    def _():
        attended = att_ref[...]
        normed = rms_scale(attended, gain_ref[...]).astype(jnp.bfloat16)
        o_ref[...] = jnp.dot(
            normed, out_w_ref[...], preferred_element_type=jnp.float32
        ).astype(o_ref.dtype)


def attention(query, key_value, out_weight, gain, tok_rows, model_width):
    lanes = 2 * HEAD
    pairs = model_width // lanes
    span = key_value.shape[0]
    past = 2 * REACH_CHIPS * tok_rows
    return pl.pallas_call(
        functools.partial(attention_kernel, tok_rows),
        grid=(pairs,),
        out_shape=jax.ShapeDtypeStruct((tok_rows, model_width), jnp.bfloat16),
        in_specs=[
            pl.BlockSpec((tok_rows, lanes), lambda h: (0, h)),
            pl.BlockSpec((span, lanes), lambda h: (0, h)),
            pl.BlockSpec((span, lanes), lambda h: (0, pairs + h)),
            pl.BlockSpec(out_weight.shape, lambda h: (0, 0)),
            pl.BlockSpec(gain.shape, lambda h: (0, 0)),
        ],
        out_specs=pl.BlockSpec((tok_rows, model_width), lambda h: (0, 0)),
        scratch_shapes=[pltpu.VMEM((tok_rows, model_width), jnp.float32)],
        compiler_params=pltpu.CompilerParams(vmem_limit_bytes=48 * 1024 * 1024),
        cost_estimate=pl.CostEstimate(
            flops=8 * tok_rows * (past + tok_rows) * model_width,
            bytes_accessed=4 * past * model_width,
            transcendentals=tok_rows * past * model_width // HEAD,
        ),
        name="window_attention",
    )(query, key_value, key_value, out_weight, gain)


def solution(mesh):
    in_specs = (
        P("fsdp", "seq", None),
        P("fsdp", "seq", None),
        P("fsdp", "seq"),
        P("seq", None),
        P(),
        P(),
        P(None, "fsdp"),
        P(None, "fsdp"),
        P(),
    )
    out_specs = P("fsdp", "seq", None)
    return jax.shard_map(local, mesh=mesh, in_specs=in_specs, out_specs=out_specs, check_vma=False)
```

```python
import functools

import jax
import jax.numpy as jnp
from jax import lax
from jax.experimental import pallas as pl
from jax.experimental.pallas import tpu as pltpu
from jax.sharding import PartitionSpec as P

HEAD = 64
WINDOW = 2048


EPSILON = 1e-05


def rms_scale(values, gain):
    return values * lax.rsqrt(jnp.mean(values * values, axis=-1, keepdims=True) + EPSILON) * gain


def local(
    dna_embed,
    site_owner,
    site_row,
    variant_table,
    norm_gain,
    conv_weight,
    qkv_weight,
    out_weight,
    attn_gain,
):
    seq_count = lax.axis_size("seq")
    tok_rows = dna_embed.shape[1]
    model_width = dna_embed.shape[2]
    slot_count = max(16, 2 * tok_rows // seq_count)
    owner_ids = site_owner[0, :, 0]
    wanted_rows = site_row[0]
    owner_onehot = (owner_ids[:, None] == jnp.arange(seq_count, dtype=jnp.int32)[None, :]).astype(
        jnp.int32
    )
    earlier_same = jnp.cumsum(owner_onehot, axis=0) - owner_onehot
    rank_within = jnp.sum(earlier_same * owner_onehot, axis=1)
    slot_index = owner_ids * slot_count + rank_within
    request_table = jnp.zeros((seq_count * slot_count,), jnp.int32).at[slot_index].set(wanted_rows)
    conv_out, full_qkv = embed_and_conv(
        jnp.broadcast_to(request_table[:, None], (seq_count * slot_count, LANES)),
        slot_index[:, None],
        dna_embed[0],
        variant_table,
        norm_gain[None, :],
        conv_weight,
        qkv_weight,
        slot_count,
    )
    query, key_value, full_out = gather_and_project(conv_out, full_qkv, out_weight)
    return attention(query, key_value, full_out, attn_gain[None, :], tok_rows, model_width)[None, :, :]


MESH = pl.DeviceIdType.MESH
CHUNKS = 4
REACH_CHIPS = 4


def window_kernel(
    count, conv_ref, weight_ref, shard_ref, query_ref, kv_ref, full_ref,
    win_ref, held_weight, held_kv, send_sem, recv_sem, swap_sem, local_sem, weight_sem, kv_sem,
):
    me = lax.axis_index("seq")
    rows = conv_ref.shape[0]
    part = rows // CHUNKS
    core = lax.rem(me, 2)
    odd = lax.rem(me // 2, 2)
    ahead = lax.rem(me + 4, count)
    behind = lax.rem(me + count - 4, count)
    beside = me + 2 - 4 * odd
    twin = me + 1 - 2 * core

    def slot(back, chunk):
        first = ((REACH_CHIPS - back) * 2 + core) * rows + chunk * part
        return win_ref.at[pl.ds(pl.multiple_of(first, part), part)]

    load_weight = pltpu.make_async_copy(weight_ref, held_weight, weight_sem)
    load_weight.start()
    own = pl.multiple_of((REACH_CHIPS * 2 + core) * rows, rows)
    win_ref[pl.ds(own, rows), :] = conv_ref[...]

    barrier = pltpu.get_barrier_semaphore()
    for other in (ahead, behind, beside, twin):
        pl.semaphore_signal(barrier, inc=1, device_id={"seq": other}, device_id_type=MESH)
    pl.semaphore_signal(
        barrier, inc=1, device_id={"fsdp": 1 - lax.axis_index("fsdp")}, device_id_type=MESH
    )
    pl.semaphore_wait(barrier, 5)
    swap = WeightSwap(shard_ref, full_ref, swap_sem, local_sem, 1)
    swap.start()

    def message(kind, chunk, source_back, target_back, target):
        return pltpu.make_async_remote_copy(
            src_ref=slot(source_back, chunk),
            dst_ref=slot(target_back, chunk),
            send_sem=send_sem.at[kind, chunk],
            recv_sem=recv_sem.at[kind, chunk],
            device_id={"seq": target},
            device_id_type=MESH,
        )

    chunks = range(CHUNKS)
    two = [message(0, j, 0, 2, ahead) for j in chunks]
    four = [message(1, j, 2, 4, ahead) for j in chunks]
    one = [message(2, j, 2 * odd, 1, beside) for j in chunks]
    three = [message(3, j, 2 + 2 * odd, 3, beside) for j in chunks]
    share = [[message(4 + back, j, back, back, twin) for j in chunks] for back in range(5)]
    width = conv_ref.shape[1]
    tile = 512
    stores = []

    def project(back, side):
        first = pl.multiple_of(((REACH_CHIPS - back) * 2 + side) * rows, rows)
        here = pl.ds(first, rows)

        def columns(index, carry):
            start = pl.multiple_of(index * tile, tile)
            held_kv[here, pl.ds(start, tile)] = jnp.dot(
                win_ref[here, :],
                held_weight[:, pl.ds(pl.multiple_of(width + start, tile), tile)],
                preferred_element_type=jnp.float32,
            ).astype(jnp.bfloat16)
            return carry

        lax.fori_loop(0, 2 * width // tile, columns, 0)
        store = pltpu.make_async_copy(held_kv.at[here], kv_ref.at[here], kv_sem.at[len(stores)])
        store.start()
        stores.append(store)

    def shared(back):
        for j in chunks:
            share[back][j].wait_recv()
        project(back, 1 - core)

    for j in chunks:
        two[j].start()
    for j in chunks:
        share[0][j].start()
    load_weight.wait()
    query_ref[...] = jnp.dot(
        conv_ref[...], held_weight[:, :width], preferred_element_type=jnp.float32
    ).astype(jnp.bfloat16)
    for j in chunks:
        two[j].wait_recv()
        four[j].start()
        one[j].start()
        share[2][j].start()
        if j == 0:
            project(0, core)
        if j == 1:
            shared(0)
    for j in chunks:
        four[j].wait_recv()
        three[j].start()
        share[4][j].start()
        one[j].wait_recv()
        share[1][j].start()
        if j == 0:
            project(2, core)
        if j == 1:
            shared(2)
    for j in chunks:
        three[j].wait_recv()
        share[3][j].start()
        if j == 0:
            project(1, core)
        if j == 1:
            project(4, core)
    shared(1)
    project(3, core)
    shared(4)
    shared(3)
    for store in stores:
        store.wait()
    for group in [two, four, one, three] + share:
        for j in chunks:
            group[j].wait_send()
    swap.finish()


def gather_and_project(conv_out, weight, shard):
    count = lax.axis_size("seq")
    rows, width = conv_out.shape
    slots = 2 * REACH_CHIPS + 2
    return pl.pallas_call(
        functools.partial(window_kernel, count),
        out_shape=[
            jax.ShapeDtypeStruct((rows, width), conv_out.dtype),
            jax.ShapeDtypeStruct((slots * rows, 2 * width), conv_out.dtype),
            jax.ShapeDtypeStruct((shard.shape[0], 2 * shard.shape[1]), shard.dtype),
        ],
        in_specs=[pl.BlockSpec(memory_space=pltpu.VMEM)] + [pl.BlockSpec(memory_space=pl.ANY)] * 2,
        out_specs=[pl.BlockSpec(memory_space=pltpu.VMEM)] + [pl.BlockSpec(memory_space=pl.ANY)] * 2,
        scratch_shapes=[
            pltpu.VMEM((slots * rows, width), conv_out.dtype),
            pltpu.VMEM(weight.shape, weight.dtype),
            pltpu.VMEM((slots * rows, 2 * width), conv_out.dtype),
            pltpu.SemaphoreType.DMA((9, CHUNKS)),
            pltpu.SemaphoreType.DMA((9, CHUNKS)),
            pltpu.SemaphoreType.DMA((4, 1)),
            pltpu.SemaphoreType.DMA,
            pltpu.SemaphoreType.DMA,
            pltpu.SemaphoreType.DMA((slots,)),
        ],
        compiler_params=pltpu.CompilerParams(
            collective_id=1, has_side_effects=True, vmem_limit_bytes=48 * 1024 * 1024
        ),
        cost_estimate=pl.CostEstimate(
            flops=4 * slots * rows * width * width,
            bytes_accessed=4 * slots * rows * width,
            transcendentals=0,
        ),
        name="gather_and_project",
    )(conv_out, weight, shard)


LANES = 128
EDGE = 16


class WeightSwap:
    def __init__(self, shard_ref, full_ref, sems, local_sem, parts):
        me = lax.axis_index("seq")
        half = lax.axis_index("fsdp")
        core = lax.rem(me, 2)
        rows, cols = shard_ref.shape
        part = rows // 2 // parts

        def block(ref, chunk, column):
            first = pl.multiple_of(core * (rows // 2) + chunk * part, part)
            return ref.at[pl.ds(first, part), pl.ds(pl.multiple_of(column * cols, LANES), cols)]

        self.own = pltpu.make_async_copy(
            shard_ref, full_ref.at[:, pl.ds(pl.multiple_of(half * cols, LANES), cols)], local_sem
        )
        self.across = [
            pltpu.make_async_remote_copy(
                src_ref=block(shard_ref, j, 0),
                dst_ref=block(full_ref, j, half),
                send_sem=sems.at[0, j],
                recv_sem=sems.at[1, j],
                device_id={"fsdp": 1 - half},
                device_id_type=MESH,
            )
            for j in range(parts)
        ]
        self.pass_on = [
            pltpu.make_async_remote_copy(
                src_ref=block(full_ref, j, 1 - half),
                dst_ref=block(full_ref, j, 1 - half),
                send_sem=sems.at[2, j],
                recv_sem=sems.at[3, j],
                device_id={"seq": me + 1 - 2 * core},
                device_id_type=MESH,
            )
            for j in range(parts)
        ]

    def start(self):
        for copy in self.across:
            copy.start()
        self.own.start()

    def finish(self):
        for arrive, give in zip(self.across, self.pass_on):
            arrive.wait_recv()
            give.start()
        self.own.wait()
        for arrive, give in zip(self.across, self.pass_on):
            arrive.wait_send()
            give.wait()


def embed_kernel(
    count, slots, request_ref, slot_ref, dna_ref, table_ref, gain_ref, taps_ref, shard_ref,
    conv_ref, full_ref,
    inbox, found, fetched, edge_out, edge_in,
    ask_send, ask_recv, give_send, give_recv, edge_sem, swap_sem, local_sem,
):
    me = lax.axis_index("seq")
    rows = dna_ref.shape[0]
    site_rows = table_ref.shape[0]
    batch = LANES // slots

    def at(ref, index):
        return ref.at[pl.ds(pl.multiple_of(index * slots, slots), slots)]

    def ask(step):
        target = lax.rem(me + step, count)
        return pltpu.make_async_remote_copy(
            src_ref=at(request_ref, target),
            dst_ref=at(inbox, step),
            send_sem=ask_send.at[step],
            recv_sem=ask_recv.at[step],
            device_id={"seq": target},
            device_id_type=MESH,
        )

    def give(step):
        return pltpu.make_async_remote_copy(
            src_ref=at(found, step),
            dst_ref=at(fetched, me),
            send_sem=give_send.at[step],
            recv_sem=give_recv.at[step],
            device_id={"seq": lax.rem(me + count - step, count)},
            device_id_type=MESH,
        )

    swap = WeightSwap(shard_ref, full_ref, swap_sem, local_sem, 2)
    barrier = pltpu.get_barrier_semaphore()

    def greet(step, carry):
        pl.semaphore_signal(
            barrier, inc=1, device_id={"seq": lax.rem(me + step, count)}, device_id_type=MESH
        )
        return carry

    lax.fori_loop(1, count, greet, 0)
    pl.semaphore_signal(
        barrier, inc=1, device_id={"fsdp": 1 - lax.axis_index("fsdp")}, device_id_type=MESH
    )
    pl.semaphore_wait(barrier, count)

    def each(first, action):
        def body(step, carry):
            action(step)
            return carry

        lax.fori_loop(first, count, body, 0)

    each(1, lambda step: ask(step).start())
    swap.start()
    inbox[0:slots, :] = request_ref[pl.ds(pl.multiple_of(me * slots, slots), slots), :]
    lane = lax.broadcasted_iota(jnp.int32, (LANES, LANES), 1)
    for group in range(count // batch):
        steps = range(group * batch, (group + 1) * batch)
        for step in steps:
            if step > 0:
                ask(step).wait_recv()
        ids = inbox[group * LANES : (group + 1) * LANES, :]
        pick = jnp.concatenate(
            [
                jnp.where(ids - base == lane, 1.0, 0.0).astype(jnp.bfloat16)
                for base in range(0, site_rows, LANES)
            ],
            axis=1,
        )
        got = jnp.dot(pick, table_ref[...], preferred_element_type=jnp.float32)
        found[group * LANES : (group + 1) * LANES, :] = got.astype(jnp.bfloat16)
        for step in steps:
            if step > 0:
                give(step).start()
    fetched[pl.ds(pl.multiple_of(me * slots, slots), slots), :] = found[0:slots, :]
    each(1, lambda step: give(step).wait_recv())

    place = lax.broadcasted_iota(jnp.int32, (rows, count * slots), 1)
    pick = jnp.where(slot_ref[...] == place, 1.0, 0.0).astype(jnp.bfloat16)
    site_embed = jnp.dot(pick, fetched[...], preferred_element_type=jnp.float32)
    resid = dna_ref[...].astype(jnp.float32) + site_embed
    normed = rms_scale(resid, gain_ref[...]).astype(jnp.bfloat16)
    edge_out[...] = normed[rows - EDGE :, :]
    edge = pltpu.make_async_remote_copy(
        src_ref=edge_out,
        dst_ref=edge_in,
        send_sem=edge_sem.at[0],
        recv_sem=edge_sem.at[1],
        device_id={"seq": lax.rem(me + 1, count)},
        device_id_type=MESH,
    )
    edge.start()
    edge.wait()
    before = jnp.where(me > 0, edge_in[...].astype(jnp.float32), 0.0)
    padded = jnp.concatenate([before, normed.astype(jnp.float32)], axis=0)
    total = jnp.zeros(dna_ref.shape, jnp.float32)
    for tap in range(taps_ref.shape[0]):
        total = total + taps_ref[tap : tap + 1, :].astype(jnp.float32) * padded[
            EDGE - tap : EDGE - tap + rows
        ]
    conv_ref[...] = total.astype(jnp.bfloat16)
    each(1, lambda step: ask(step).wait_send())
    each(1, lambda step: give(step).wait_send())
    swap.finish()


def embed_and_conv(requests, slot_index, dna, table, gain, taps, shard, slots):
    count = lax.axis_size("seq")
    rows, width = dna.shape
    vmem = pl.BlockSpec(memory_space=pltpu.VMEM)
    anywhere = pl.BlockSpec(memory_space=pl.ANY)
    dma = pltpu.SemaphoreType.DMA
    return pl.pallas_call(
        functools.partial(embed_kernel, count, slots),
        out_shape=[
            jax.ShapeDtypeStruct((rows, width), jnp.bfloat16),
            jax.ShapeDtypeStruct((shard.shape[0], 2 * shard.shape[1]), shard.dtype),
        ],
        in_specs=[vmem] * 6 + [anywhere],
        out_specs=[vmem, anywhere],
        scratch_shapes=[
            pltpu.VMEM((count * slots, LANES), jnp.int32),
            pltpu.VMEM((count * slots, width), jnp.bfloat16),
            pltpu.VMEM((count * slots, width), jnp.bfloat16),
            pltpu.VMEM((EDGE, width), jnp.bfloat16),
            pltpu.VMEM((EDGE, width), jnp.bfloat16),
            dma((count,)),
            dma((count,)),
            dma((count,)),
            dma((count,)),
            dma((2,)),
            dma((4, 2)),
            dma,
        ],
        compiler_params=pltpu.CompilerParams(
            collective_id=2, has_side_effects=True, vmem_limit_bytes=48 * 1024 * 1024
        ),
        cost_estimate=pl.CostEstimate(
            flops=4 * rows * table.size, bytes_accessed=2 * table.size, transcendentals=0
        ),
        name="embed_and_conv",
    )(requests, slot_index, dna, table, gain, taps, shard)


def attention_kernel(tok_rows, q_ref, k_ref, v_ref, out_w_ref, gain_ref, o_ref, att_ref):
    pair = pl.program_id(0)
    pairs = pl.num_programs(0)
    rank = lax.axis_index("seq")
    past = 2 * REACH_CHIPS * tok_rows
    shift = pl.multiple_of(lax.rem(rank, 2) * tok_rows, tok_rows)
    old = pl.ds(shift, tok_rows)
    mid = pl.ds(pl.multiple_of(shift + tok_rows, tok_rows), past - tok_rows)
    new = pl.ds(pl.multiple_of(shift + past, tok_rows), tok_rows)
    lanes = q_ref.shape[1]
    low_half = lax.broadcasted_iota(jnp.int32, (tok_rows, lanes), 1) < HEAD
    row = lax.broadcasted_iota(jnp.int32, (tok_rows, tok_rows), 0)
    col = lax.broadcasted_iota(jnp.int32, (tok_rows, tok_rows), 1)
    recent = col <= row
    absent = past - rank * tok_rows
    mid_col = tok_rows + lax.broadcasted_iota(jnp.int32, (tok_rows, past - tok_rows), 1)
    query = q_ref[...]
    scaled = query * jnp.asarray(HEAD ** (-0.5), query.dtype)
    nt = (((1,), (1,)), ((), ()))
    halves = []
    for half in range(2):
        keep = low_half if half == 0 else jnp.logical_not(low_half)
        q_head = jnp.where(keep, scaled, jnp.zeros_like(scaled))
        s_mid = lax.dot_general(q_head, k_ref[mid, :], nt, preferred_element_type=jnp.float32)
        s_old = lax.dot_general(q_head, k_ref[old, :], nt, preferred_element_type=jnp.float32)
        s_new = lax.dot_general(q_head, k_ref[new, :], nt, preferred_element_type=jnp.float32)
        s_mid = jnp.where(mid_col >= absent, s_mid, -jnp.inf)
        s_old = jnp.where(col >= absent, s_old, -jnp.inf)
        s_edge = jnp.where(recent, s_new, s_old)
        highest = jnp.maximum(
            jnp.max(s_mid, axis=-1, keepdims=True), jnp.max(s_edge, axis=-1, keepdims=True)
        )
        e_mid = jnp.exp(s_mid - highest)
        e_edge = jnp.exp(s_edge - highest)
        total = jnp.sum(e_mid, axis=-1, keepdims=True) + jnp.sum(e_edge, axis=-1, keepdims=True)
        inverse = 1.0 / total
        p_mid = (e_mid * inverse).astype(jnp.bfloat16)
        p_edge = e_edge * inverse
        p_new = jnp.where(recent, p_edge, 0.0).astype(jnp.bfloat16)
        p_old = jnp.where(recent, 0.0, p_edge).astype(jnp.bfloat16)
        halves.append(
            jnp.dot(p_mid, v_ref[mid, :], preferred_element_type=jnp.float32)
            + jnp.dot(p_old, v_ref[old, :], preferred_element_type=jnp.float32)
            + jnp.dot(p_new, v_ref[new, :], preferred_element_type=jnp.float32)
        )
    att_ref[:, pl.ds(pl.multiple_of(pair * lanes, lanes), lanes)] = jnp.where(
        low_half, halves[0], halves[1]
    )

    @pl.when(pair == pairs - 1)
    def _():
        attended = att_ref[...]
        normed = rms_scale(attended, gain_ref[...]).astype(jnp.bfloat16)
        o_ref[...] = jnp.dot(
            normed, out_w_ref[...], preferred_element_type=jnp.float32
        ).astype(o_ref.dtype)


def attention(query, key_value, out_weight, gain, tok_rows, model_width):
    lanes = 2 * HEAD
    pairs = model_width // lanes
    span = key_value.shape[0]
    past = 2 * REACH_CHIPS * tok_rows
    return pl.pallas_call(
        functools.partial(attention_kernel, tok_rows),
        grid=(pairs,),
        out_shape=jax.ShapeDtypeStruct((tok_rows, model_width), jnp.bfloat16),
        in_specs=[
            pl.BlockSpec((tok_rows, lanes), lambda h: (0, h)),
            pl.BlockSpec((span, lanes), lambda h: (0, h)),
            pl.BlockSpec((span, lanes), lambda h: (0, pairs + h)),
            pl.BlockSpec(out_weight.shape, lambda h: (0, 0)),
            pl.BlockSpec(gain.shape, lambda h: (0, 0)),
        ],
        out_specs=pl.BlockSpec((tok_rows, model_width), lambda h: (0, 0)),
        scratch_shapes=[pltpu.VMEM((tok_rows, model_width), jnp.float32)],
        compiler_params=pltpu.CompilerParams(vmem_limit_bytes=48 * 1024 * 1024),
        cost_estimate=pl.CostEstimate(
            flops=8 * tok_rows * (past + tok_rows) * model_width,
            bytes_accessed=4 * past * model_width,
            transcendentals=tok_rows * past * model_width // HEAD,
        ),
        name="window_attention",
    )(query, key_value, key_value, out_weight, gain)


def solution(mesh):
    in_specs = (
        P("fsdp", "seq", None),
        P("fsdp", "seq", None),
        P("fsdp", "seq"),
        P("seq", None),
        P(),
        P(),
        P(None, "fsdp"),
        P(None, "fsdp"),
        P(),
    )
    out_specs = P("fsdp", "seq", None)
    return jax.shard_map(local, mesh=mesh, in_specs=in_specs, out_specs=out_specs, check_vma=False)
```
